32 devices in a mesh: wide: 8 (over y, x, core), narrow: 4 (over z).
Axes of the slice: x: 2, y: 2, z: 4, core: 2. Of those that a mesh axis runs over, the one named last changes fastest.
Arguments:
- features: bfloat16 [131072, 602], P(('wide', 'narrow')), may hold values from -6 to 6
- tile_src: int32 [1024, 12], P(('wide', 'narrow')), may hold values from 0 to 33, as said below
- edge_weight: bfloat16 [1024, 12, 128, 128], P(('wide', 'narrow')), may hold values from -0.044189453 to 0.044189453
- send_lists: int32 [32, 32, 8], P(('wide', 'narrow')), may hold values from -1 to 4095, as said below
- labels: int32 [131072], P(('wide', 'narrow')), may hold values from 0 to 40
- train_mask: int32 [131072], P(('wide', 'narrow')), may hold values from 0 to 1, as said below
- w_in: float32 [602, 512], replicated, may hold values from -0.25 to 0.25
- w_pair: float32 [1, 2, 512, 512], replicated, may hold values from -0.25 to 0.25
- w_cat: float32 [1, 1024, 512], replicated, may hold values from -0.1875 to 0.1875
- w_out: float32 [512, 41], replicated, may hold values from -0.25 to 0.25
- m_in: float32 [602, 512], replicated, may hold values from -2.861023e-06 to 2.861023e-06
- m_pair: float32 [1, 2, 512, 512], replicated, may hold values from -2.861023e-06 to 2.861023e-06
- m_cat: float32 [1, 1024, 512], replicated, may hold values from -2.861023e-06 to 2.861023e-06
- m_out: float32 [512, 41], replicated, may hold values from -2.861023e-06 to 2.861023e-06
- v_in: float32 [602, 512], replicated, may hold values from 2.903196e-15 to 1.1612784e-14
- v_pair: float32 [1, 2, 512, 512], replicated, may hold values from 2.903196e-15 to 1.1612784e-14
- v_cat: float32 [1, 1024, 512], replicated, may hold values from 2.903196e-15 to 1.1612784e-14
- v_out: float32 [512, 41], replicated, may hold values from 2.903196e-15 to 1.1612784e-14
Outputs:
- new_w_in: float32 [602, 512], replicated
- new_w_pair: float32 [1, 2, 512, 512], replicated
- new_w_cat: float32 [1, 1024, 512], replicated
- new_w_out: float32 [512, 41], replicated
- new_m_in: float32 [602, 512], replicated
- new_m_pair: float32 [1, 2, 512, 512], replicated
- new_m_cat: float32 [1, 1024, 512], replicated
- new_m_out: float32 [512, 41], replicated
- new_v_in: float32 [602, 512], replicated
- new_v_pair: float32 [1, 2, 512, 512], replicated
- new_v_cat: float32 [1, 1024, 512], replicated
- new_v_out: float32 [512, 41], replicated
- loss_sum: float32 [], replicated
- train_count: float32 [], replicated
- grad_norm: float32 [], replicated
The draws below stay inside these ranges and needn't reach their ends.
Inputs may be any that keep to these rules, and one draw needn't show every extreme that they name: `send_lists`: entry [q, p, s] is one of device q's 4096 owned rows (numbered from 0) that device q sends to device p in slot s, or -1 for an empty slot; empty slots stand after used ones; each list has 1 to 8 used slots, and every device has a full list. `tile_src`: entries index the 34 blocks of the owning device's rows followed by its received rows in order of sending device and slot; every block is named on every device. `train_mask`: node 0 is a training node.
All inputs are finite; a program needn't handle non-finite values.
Results may differ from the reference program's by a relative error of at most 0.018.
Values may be sent and summed in bfloat16 or wider, within the bound.
No kernel may reach another device: no remote copies, remote signals or barrier semaphores. Data moves between devices by JAX's collectives and lax.ppermute only.
A program may use at most 192 MiB of HBM per device.

```python
import jax
import jax.numpy as jnp
from jax import lax

F_IN = 602
H = 512
CLASSES = 41
LAYERS = 1
NODE_DEV = 4096
TILE = 128
KT = 12
HALO_PEER = 8
ADAM_STEP = 10
WIDE_COUNT = 8
NARROW_COUNT = 4
PEERS = 32
NODES = 131072
NB = 32
NBX = 34
NPARAM = 1377792


def draw_send_lists(key, part):
    key = jax.random.fold_in(key, 11)
    count_key, row_key = jax.random.split(key)
    owners = jnp.arange(PEERS, dtype=jnp.int32)[:, None]
    targets = jnp.arange(PEERS, dtype=jnp.int32)[None, :]
    counts = jax.random.randint(count_key, (PEERS, PEERS), 1, HALO_PEER + 1)
    counts = jnp.where(targets == (owners + 1) % PEERS, HALO_PEER, counts)
    chosen = jax.random.randint(row_key, (PEERS, PEERS, HALO_PEER), 0, NODE_DEV)
    slot_index = jnp.arange(HALO_PEER, dtype=jnp.int32)
    return jnp.where(slot_index[None, None, :] < counts[:, :, None], chosen, -1).astype(jnp.int32)


def draw_tile_src(key, part):
    key = jax.random.fold_in(key, 12)
    halo_blocks = NBX - NB
    half_count = KT // 2
    block_index = (jnp.arange(PEERS * NB, dtype=jnp.int32) % NB)[:, None]
    column = jnp.arange(KT, dtype=jnp.int32)[None, :]
    random_pick = jax.random.randint(key, (PEERS * NB, KT), 0, NBX)
    cycled = NB + (block_index * half_count + column + halo_blocks - 1) % halo_blocks
    picked = jnp.where(column == 0, block_index, jnp.where(column <= half_count, cycled, random_pick))
    return picked.astype(jnp.int32)


def draw_train_mask(key, part):
    key = jax.random.fold_in(key, 13)
    row_index = jnp.arange(NODES, dtype=jnp.int32)
    device = row_index // NODE_DEV
    wide_pos = device // NARROW_COUNT
    narrow_pos = device % NARROW_COUNT
    spread = (WIDE_COUNT - 1) * (NARROW_COUNT - 1)
    chance = 8 * (WIDE_COUNT - 1 + 2 * wide_pos) * (NARROW_COUNT - 1 + 2 * narrow_pos)
    rolled = jax.random.randint(key, (NODES,), 0, 100 * spread)
    return jnp.where((rolled < chance) | (row_index == 0), 1, 0).astype(jnp.int32)


def set_ends(entries, stream_key, smallest, top_value):
    dims = entries.shape
    index_at = [jax.random.randint(jax.random.fold_in(stream_key, axis), (), 0, dims[axis]) for axis in range(len(dims))]
    entries = entries.at[tuple(index_at)].set(smallest)
    longest = dims.index(max(dims))
    index_at[longest] = (index_at[longest] + 1) % dims[longest]
    return entries.at[tuple(index_at)].set(top_value)


def levels(key, dims, cuts, least, largest):
    loudness = 1.0
    for axis_at, blocks in cuts:
        draws = jax.random.uniform(jax.random.fold_in(jax.random.fold_in(key, 6), axis_at), (blocks,), jnp.float32, least / len(cuts), largest / len(cuts))
        loudness = loudness * jnp.repeat(jnp.exp(draws), dims[axis_at] // blocks).reshape((-1,) + (1,) * (len(dims) - 1 - axis_at))
    return loudness


def noise(stream_key, extent, scale, limit, cuts=(), kind=jnp.bfloat16):
    drawn = jax.random.normal(stream_key, extent, jnp.float32) * scale
    if len(cuts) > 0:
        drawn = levels(stream_key, extent, cuts, -0.22, 0.18) * drawn
    return jnp.clip(drawn, min=-limit, max=limit).astype(kind)


def setup_inputs(seed: int = 0) -> dict:
    seeds = jax.random.split(jax.random.key(seed), 19)
    features = noise(seeds[0], (NODES, F_IN), 1.0, 6.0, ((0, 32),))
    tile_src = draw_tile_src(jax.random.fold_in(seeds[18], 71), 0)
    edge_weight = jnp.clip(jax.random.uniform(seeds[2], (PEERS * NB, KT, TILE, TILE), jnp.float32, -0.044189453, 0.044189453) * levels(seeds[2], (PEERS * NB, KT, TILE, TILE), ((0, 32),), -0.4, 0.0), -0.044189453, 0.044189453).astype(jnp.bfloat16)
    send_lists = draw_send_lists(jax.random.fold_in(seeds[18], 71), 0)
    labels = set_ends(jax.random.randint(seeds[4], (NODES,), 0, CLASSES), jax.random.fold_in(seeds[4], 1), 0, CLASSES - 1).astype(jnp.int32)
    train_mask = draw_train_mask(jax.random.fold_in(seeds[18], 71), 0)
    w_in = noise(seeds[6], (F_IN, H), F_IN ** -0.5, 0.25, (), jnp.float32)
    w_pair = noise(seeds[7], (LAYERS, 2, H, H), H ** -0.5, 0.25, (), jnp.float32)
    w_cat = noise(seeds[8], (LAYERS, 2 * H, H), (2 * H) ** -0.5, 0.1875, (), jnp.float32)
    w_out = noise(seeds[9], (H, CLASSES), H ** -0.5, 0.25, (), jnp.float32)
    m_in = noise(seeds[10], (F_IN, H), (0.000222 / NPARAM ** 0.5), 2.86102294921875e-06, (), jnp.float32)
    m_pair = noise(seeds[11], (LAYERS, 2, H, H), (0.000222 / NPARAM ** 0.5), 2.86102294921875e-06, (), jnp.float32)
    m_cat = noise(seeds[12], (LAYERS, 2 * H, H), (0.000222 / NPARAM ** 0.5), 2.86102294921875e-06, (), jnp.float32)
    m_out = noise(seeds[13], (H, CLASSES), (0.000222 / NPARAM ** 0.5), 2.86102294921875e-06, (), jnp.float32)
    v_in = jnp.clip(jax.random.uniform(seeds[14], (F_IN, H), jnp.float32, 2.9031958975934578e-15, 1.1612783590373831e-14), 2.9031958975934578e-15, 1.1612783590373831e-14)
    v_pair = jnp.clip(jax.random.uniform(seeds[15], (LAYERS, 2, H, H), jnp.float32, 2.9031958975934578e-15, 1.1612783590373831e-14), 2.9031958975934578e-15, 1.1612783590373831e-14)
    v_cat = jnp.clip(jax.random.uniform(seeds[16], (LAYERS, 2 * H, H), jnp.float32, 2.9031958975934578e-15, 1.1612783590373831e-14), 2.9031958975934578e-15, 1.1612783590373831e-14)
    v_out = jnp.clip(jax.random.uniform(seeds[17], (H, CLASSES), jnp.float32, 2.9031958975934578e-15, 1.1612783590373831e-14), 2.9031958975934578e-15, 1.1612783590373831e-14)
    return dict(features=features, tile_src=tile_src, edge_weight=edge_weight, send_lists=send_lists, labels=labels, train_mask=train_mask, w_in=w_in, w_pair=w_pair, w_cat=w_cat, w_out=w_out, m_in=m_in, m_pair=m_pair, m_cat=m_cat, m_out=m_out, v_in=v_in, v_pair=v_pair, v_cat=v_cat, v_out=v_out)


@jax.custom_vjp
def low(v):
    return lax.optimization_barrier(v.astype(jnp.bfloat16)).astype(jnp.float32)

@jax.custom_vjp
def low_back(v):
    return v

def low_keep(v):
    return (low(v), None)

def low_pass(kept, grad):
    return (grad,)

def back_keep(v):
    return (v, None)

def back_low(kept, grad):
    return (low(grad),)
low.defvjp(low_keep, low_pass)
low_back.defvjp(back_keep, back_low)
HIGHEST = lax.Precision.HIGHEST
NORM_EPS = 1e-06
SMOOTHING = 0.1
CLIP_AT = 0.002
LEARN_RATE = 0.05
BETA_FIRST = 0.9
BETA_SECOND = 0.999
ADAM_EPS = 1e-08
WEIGHT_DECAY = 0.01

def adam_update(weight, grad, first, second):
    first_new = BETA_FIRST * first + (1.0 - BETA_FIRST) * grad
    second_new = BETA_SECOND * second + (1.0 - BETA_SECOND) * grad * grad
    first_hat = first_new / (1.0 - BETA_FIRST ** ADAM_STEP)
    second_hat = second_new / (1.0 - BETA_SECOND ** ADAM_STEP)
    weight_new = weight - LEARN_RATE * (first_hat / (jnp.sqrt(second_hat) + ADAM_EPS) + WEIGHT_DECAY * weight)
    return (first_new, second_new, weight_new)

def halo_rows(hidden, slot_lists):

    def from_owner(owner_rows, owner_lists):
        picked = jnp.take(owner_rows, jnp.clip(owner_lists, 0, NODE_DEV - 1), axis=0)
        return jnp.where((owner_lists >= 0)[..., None], picked, 0.0)
    outgoing = jax.vmap(from_owner)(hidden, slot_lists)
    return jnp.transpose(outgoing, (1, 0, 2, 3)).reshape(PEERS, PEERS * HALO_PEER, H)

def layer_device(inputs_dev, halo_dev, sources, edge_vals, pair_now, cat_now):
    extended = jnp.concatenate([inputs_dev, halo_dev], axis=0).reshape(NBX, TILE, H)
    gathered = jnp.take(extended, sources, axis=0)
    summed = jnp.einsum('bkij,bkjh->bih', edge_vals, gathered, precision=HIGHEST).reshape(NODE_DEV, H)
    aggregate = low(low_back(summed))
    own_part = jnp.dot(inputs_dev, pair_now[0], precision=HIGHEST)
    neighbour = jnp.dot(aggregate, pair_now[1], precision=HIGHEST)
    joined = low(low_back(jnp.concatenate([own_part, neighbour], axis=1)))
    mixed = low_back(jnp.dot(joined, cat_now, precision=HIGHEST))
    active = jax.nn.gelu(mixed, approximate=True)
    return active * lax.rsqrt(lax.optimization_barrier(jnp.mean(active * active, axis=1, keepdims=True)) + NORM_EPS)

def forward(w_in, w_pair, w_cat, w_out, node_feats, sources, edge_vals, slot_lists, targets, mask_vals, total):
    first = jnp.einsum('dnf,fh->dnh', node_feats, w_in, precision=HIGHEST)
    hidden = low(low_back(first))
    for layer_index in range(LAYERS):
        halo = halo_rows(hidden, slot_lists)
        pair_now = w_pair[layer_index]
        cat_now = w_cat[layer_index]

        def one_device(packed):
            return layer_device(packed[0], packed[1], packed[2], packed[3], pair_now, cat_now)
        hidden = low(lax.map(jax.checkpoint(one_device), (hidden, halo, sources, edge_vals)))
    logits = low_back(jnp.einsum('dnh,hc->dnc', hidden, w_out, precision=HIGHEST))
    log_prob = jax.nn.log_softmax(logits, axis=-1)
    smoothed = (1.0 - SMOOTHING) * jax.nn.one_hot(targets, CLASSES, dtype=log_prob.dtype) + SMOOTHING / CLASSES
    per_node = -lax.optimization_barrier(jnp.sum(smoothed * log_prob, axis=-1))
    loss_sum = jnp.sum(per_node * mask_vals)
    return (loss_sum / total, loss_sum)

def reference(features, tile_src, edge_weight, send_lists, labels, train_mask, w_in, w_pair, w_cat, w_out, m_in, m_pair, m_cat, m_out, v_in, v_pair, v_cat, v_out):
    node_feats = features.astype(jnp.float32).reshape(PEERS, NODE_DEV, F_IN)
    sources = tile_src.reshape(PEERS, NB, KT).astype(jnp.int32)
    edge_vals = edge_weight.astype(jnp.float32).reshape(PEERS, NB, KT, TILE, TILE)
    targets = labels.reshape(PEERS, NODE_DEV)
    mask_vals = train_mask.astype(jnp.float32).reshape(PEERS, NODE_DEV)
    train_count = jnp.sum(mask_vals)

    def loss_of(wa, wb, wc, wd):
        return forward(wa, wb, wc, wd, node_feats, sources, edge_vals, send_lists, targets, mask_vals, train_count)
    loss_value, pull, loss_sum = jax.vjp(loss_of, w_in, w_pair, w_cat, w_out, has_aux=True)
    grads = pull(jnp.ones_like(loss_value))
    squares = jnp.sum(grads[0] * grads[0]) + jnp.sum(grads[1] * grads[1]) + jnp.sum(grads[2] * grads[2]) + jnp.sum(grads[3] * grads[3])
    grad_norm = jnp.sqrt(squares)
    scale = CLIP_AT / jnp.maximum(grad_norm, CLIP_AT)
    m_in_n, v_in_n, w_in_n = adam_update(w_in, grads[0] * scale, m_in, v_in)
    m_pair_n, v_pair_n, w_pair_n = adam_update(w_pair, grads[1] * scale, m_pair, v_pair)
    m_cat_n, v_cat_n, w_cat_n = adam_update(w_cat, grads[2] * scale, m_cat, v_cat)
    m_out_n, v_out_n, w_out_n = adam_update(w_out, grads[3] * scale, m_out, v_out)
    return (w_in_n, w_pair_n, w_cat_n, w_out_n, m_in_n, m_pair_n, m_cat_n, m_out_n, v_in_n, v_pair_n, v_cat_n, v_out_n, loss_sum, train_count, grad_norm)
```

```python
import functools

import jax
import jax.numpy as jnp
from jax import lax
from jax.experimental import pallas as pl
from jax.experimental.pallas import tpu as pltpu
from jax.sharding import PartitionSpec as P

ADAM_STEP = 10
NORM_EPS = 1e-06
SMOOTHING = 0.1
CLIP_AT = 0.002
LEARN_RATE = 0.05
BETA_FIRST = 0.9
BETA_SECOND = 0.999
ADAM_EPS = 1e-08
WEIGHT_DECAY = 0.01

AXES = ("wide", "narrow")
LANES = 128
TAIL = 8
GELU_A = 0.7978845608028654
GELU_B = 0.044715
F32 = jnp.float32
BF16 = jnp.bfloat16
VMEM_LIMIT = 58 * 1024 * 1024


def mm(left, right):
    return jnp.dot(left, right, preferred_element_type=F32)


def mm_nt(left, right):
    return lax.dot_general(left, right, (((1,), (1,)), ((), ())), preferred_element_type=F32)


def mm_tn(left, right):
    return lax.dot_general(left, right, (((0,), (0,)), ((), ())), preferred_element_type=F32)


def split_tail(rows, is_last):
    tail = rows[-TAIL:]
    total = tail + pltpu.roll(tail, TAIL - 1, 0)
    high = total.astype(BF16).astype(F32)
    low = pltpu.roll(total - high, 1, 0)
    even = lax.broadcasted_iota(jnp.int32, tail.shape, 0) % 2 == 0
    tail = jnp.where(is_last, jnp.where(even, high, low), tail)
    return jnp.concatenate([rows[:-TAIL], tail], axis=0).astype(BF16)


def weights_kernel(w_in, w_pair, w_cat, w_out, big, prod, in_t, pair_t, cat_b, out_b):
    fan_in, hidden = w_in.shape
    padded = big.shape[0] // 2
    classes = w_out.shape[1]
    in_b = jnp.concatenate(
        [w_in[...].astype(BF16), jnp.zeros((padded - fan_in, hidden), BF16)], axis=0
    )
    in_t[...] = in_b.T
    cat_b[...] = w_cat[...].astype(BF16)
    out_b[...] = jnp.concatenate(
        [w_out[...].astype(BF16), jnp.zeros((hidden, LANES - classes), BF16)], axis=1
    )
    for side in range(2):
        pair_b = w_pair[side].astype(BF16)
        pair_t[side] = pair_b.T
        both = mm(pair_b, cat_b[side * hidden : (side + 1) * hidden, :]).astype(BF16)
        prod[side] = both
        big[side * padded : (side + 1) * padded, :] = mm(in_b, both).astype(BF16)


def weight_products(w_in, w_pair, w_cat, w_out, padded):
    hidden = w_in.shape[1]
    shapes = (
        (2 * padded, hidden),
        (2, hidden, hidden),
        (hidden, padded),
        (2, hidden, hidden),
        (2 * hidden, hidden),
        (hidden, LANES),
    )
    return pl.pallas_call(
        weights_kernel,
        out_shape=[jax.ShapeDtypeStruct(s, BF16) for s in shapes],
        compiler_params=pltpu.CompilerParams(vmem_limit_bytes=VMEM_LIMIT),
        cost_estimate=pl.CostEstimate(
            flops=4 * hidden * hidden * (hidden + padded),
            bytes_accessed=12 * 1024 * 1024,
            transcendentals=0,
        ),
        name="weight_products",
    )(w_in, w_pair, w_cat, w_out)


def nodes_kernel(
    geometry,
    src,
    me,
    feat,
    halo,
    edge,
    labels,
    mask,
    big,
    out_b,
    keep,
    send,
    ext,
    acc,
    acc_out,
    acc_loss,
):
    fan_in, classes, steps = geometry
    nb, tile, padded = ext.shape[0] - halo.shape[0] // ext.shape[1], ext.shape[1], ext.shape[2]
    per_step, kt = edge.shape[0], edge.shape[1]
    rows = per_step * tile
    hidden = big.shape[1]
    step = pl.program_id(0)

    @pl.when(step == 0)
    def _():
        zeros = jnp.zeros((tile, padded - fan_in), BF16)

        def fill(block, carry):
            own = feat[pl.ds(pl.multiple_of(block * tile, tile), tile), :]
            ext[block] = jnp.concatenate([own, zeros], axis=1)
            return carry

        lax.fori_loop(0, nb, fill, 0)
        for block in range(halo.shape[0] // tile):
            ext[nb + block] = halo[block * tile : (block + 1) * tile, :]
        acc[...] = jnp.zeros_like(acc)
        acc_out[...] = jnp.zeros_like(acc_out)
        acc_loss[...] = jnp.zeros_like(acc_loss)

    sums = []
    for j in range(per_step):
        block = step * per_step + j
        gathered = jnp.concatenate([ext[src[block * kt + k]] for k in range(kt)], axis=0)
        weights = jnp.concatenate([edge[j, k] for k in range(kt)], axis=1)
        sums.append(mm(weights, gathered).astype(BF16))
    own = ext[pl.ds(step * per_step, per_step)].reshape(rows, padded)
    both = jnp.concatenate([own, jnp.concatenate(sums, axis=0)], axis=1)
    mixed = mm(both, big[...])
    square = mixed * mixed
    curve = jnp.tanh(mixed * (GELU_A + (GELU_A * GELU_B) * square))
    half = 0.5 + 0.5 * curve
    active = mixed * half
    slope = half + (0.5 * mixed) * (1.0 - curve * curve) * (
        GELU_A + (3.0 * GELU_A * GELU_B) * square
    )
    inverse = lax.rsqrt(jnp.sum(active * active, axis=1, keepdims=True) / hidden + NORM_EPS)
    top = (active * inverse).astype(BF16)
    logits = mm(top, out_b[...])
    lane = lax.broadcasted_iota(jnp.int32, (rows, LANES), 1)
    logits = jnp.where(lane < classes, logits, -1e30)
    logits = logits - jnp.max(logits, axis=1, keepdims=True)
    powers = jnp.exp(logits)
    total = jnp.sum(powers, axis=1, keepdims=True)
    sub = lax.broadcasted_iota(jnp.int32, (LANES, tile), 0)
    turned = []
    for j in range(per_step):
        block = step * per_step + j
        hot = (sub == labels[pl.ds(block, 1), :]).astype(F32)
        hot = jnp.where(sub == LANES - 1, mask[pl.ds(block, 1), :].astype(F32), hot)
        turned.append(hot.T)
    turned = jnp.concatenate(turned, axis=0)
    used = turned[:, LANES - 1 :]
    target = jnp.where(
        lane < classes, (1.0 - SMOOTHING) * turned + SMOOTHING / classes, 0.0
    )
    loss = -(target * (logits - jnp.log(total))) * used
    acc_loss[0:1, :] += jnp.sum(loss, axis=0, keepdims=True)
    acc_loss[1:2, :] += jnp.sum(jnp.where(lane == 0, used, 0.0), axis=0, keepdims=True)
    grad_logits = ((powers / total - target) * used).astype(BF16)
    acc_out[...] += mm_tn(grad_logits, top)
    grad_top = mm_nt(grad_logits, out_b[...])
    along = jnp.sum(active * grad_top, axis=1, keepdims=True)
    pull = inverse * inverse * inverse * along / hidden
    grad_mixed = ((inverse * grad_top - active * pull) * slope).astype(BF16)
    acc[...] += mm_tn(both, grad_mixed)

    @pl.when(step == steps - 1)
    def _():
        first = padded - fan_in
        acc[fan_in:padded, :] = acc_out[:first, :]
        acc[padded + fan_in : padded + fan_in + classes - first, :] = acc_out[first:classes, :]
        row = lax.broadcasted_iota(jnp.int32, (TAIL, hidden), 0)
        loss_sum = jnp.sum(acc_loss[0:1, :])
        count = jnp.sum(acc_loss[1:2, :])
        tail = jnp.where(row == 0, loss_sum, jnp.where(row == 2, count, 0.0))
        acc[2 * padded - TAIL :, :] = tail
        core = me[0]
        pieces, piece = keep.shape[0], keep.shape[1]
        for p in range(pieces):
            mine = pl.multiple_of(core * padded + p * piece, TAIL)
            other = pl.multiple_of((1 - core) * padded + p * piece, TAIL)
            keep[p] = acc[pl.ds(mine, piece), :]
            is_last = jnp.logical_and(core == 0, p == pieces - 1)
            send[p] = split_tail(acc[pl.ds(other, piece), :], is_last)


def node_pass(src, me, feat, halo, edge, labels, mask, big, out_b, classes, pieces):
    nodes, fan_in = feat.shape
    nb, kt, tile, _ = edge.shape
    padded = halo.shape[1]
    hidden = big.shape[1]
    per_step = 4
    steps = nb // per_step
    piece = padded // pieces
    once = pl.Buffered(buffer_count=1)
    full = lambda shape: pl.BlockSpec(shape, lambda i, *_: (0,) * len(shape), pipeline_mode=once)
    out_full = lambda shape: pl.BlockSpec(shape, lambda i, *_: (0,) * len(shape))
    return pl.pallas_call(
        functools.partial(nodes_kernel, (fan_in, classes, steps)),
        out_shape=[
            jax.ShapeDtypeStruct((pieces, piece, hidden), F32),
            jax.ShapeDtypeStruct((pieces, piece, hidden), BF16),
        ],
        grid_spec=pltpu.PrefetchScalarGridSpec(
            num_scalar_prefetch=2,
            grid=(steps,),
            in_specs=[
                full((nodes, fan_in)),
                full(halo.shape),
                pl.BlockSpec((per_step, kt, tile, tile), lambda i, *_: (i, 0, 0, 0)),
                full(labels.shape),
                full(mask.shape),
                full(big.shape),
                full(out_b.shape),
            ],
            out_specs=[out_full((pieces, piece, hidden))] * 2,
            scratch_shapes=[
                pltpu.VMEM((nb + halo.shape[0] // tile, tile, padded), BF16),
                pltpu.VMEM((2 * padded, hidden), F32),
                pltpu.VMEM((LANES, hidden), F32),
                pltpu.VMEM((TAIL, LANES), F32),
            ],
        ),
        compiler_params=pltpu.CompilerParams(
            vmem_limit_bytes=VMEM_LIMIT, dimension_semantics=("arbitrary",)
        ),
        name="node_pass",
    )(src, me, feat, halo, edge, labels, mask, big, out_b)


def pair_sum_kernel(me, keep, got, own, *outs):
    pieces = keep.shape[0]
    core, plane = me[0], me[1]
    own[...] = keep[plane] + got[plane].astype(F32)
    for d in range(1, pieces):
        p = plane ^ d
        total = keep[p] + got[p].astype(F32)
        outs[d - 1][...] = split_tail(total, jnp.logical_and(core == 1, p == pieces - 1))


def plane_sum_kernel(pieces, me, own, *refs):
    total = own[...]
    for ref in refs[:-1]:
        total = total + ref[...].astype(F32)
    is_last = jnp.logical_and(me[0] == 1, me[1] == pieces - 1)
    refs[-1][...] = split_tail(total, is_last)


def line_sum_kernel(pieces, me, *refs):
    parts = [ref[...].astype(F32) for ref in refs[:-1]]
    while len(parts) > 1:
        parts = [parts[i] + parts[i + 1] for i in range(0, len(parts), 2)]
    is_last = jnp.logical_and(me[0] == 1, me[1] == pieces - 1)
    refs[-1][...] = split_tail(parts[0], is_last)


def small_call(kernel, me, operands, shapes, name):
    spec = pl.BlockSpec(memory_space=pltpu.VMEM)
    return pl.pallas_call(
        kernel,
        out_shape=shapes,
        in_specs=[pl.BlockSpec(memory_space=pltpu.SMEM)] + [spec] * len(operands),
        out_specs=[spec] * len(shapes),
        compiler_params=pltpu.CompilerParams(vmem_limit_bytes=VMEM_LIMIT),
        name=name,
    )(me, *operands)


def update_kernel(geometry, me, *refs):
    fan_in, classes, pieces = geometry
    got = refs[: 2 * pieces]
    prod, in_t, pair_t, cat_b = refs[2 * pieces : 2 * pieces + 4]
    states = refs[2 * pieces + 4 : 2 * pieces + 16]
    news = refs[2 * pieces + 16 : 2 * pieces + 28]
    loss_out, count_out, norm_out = refs[2 * pieces + 28 : 2 * pieces + 31]
    rest = refs[2 * pieces + 31 :]
    bufs = rest[:12]
    summed, g_in, g_pair, g_cat, g_out, sems_in, sems_out = rest[12:]
    hidden = prod.shape[1]
    padded = in_t.shape[1]
    core, plane = me[0], me[1]
    loads = [pltpu.make_async_copy(states[n], bufs[n], sems_in.at[n]) for n in range(12)]
    for load in loads:
        load.start()
    piece = padded // pieces
    for d in range(pieces):
        at = (plane ^ d) * piece
        mine = pl.multiple_of(core * padded + at, TAIL)
        other = pl.multiple_of((1 - core) * padded + at, TAIL)
        summed[pl.ds(mine, piece), :] = got[d][...].astype(F32)
        summed[pl.ds(other, piece), :] = got[pieces + d][...].astype(F32)
    first = padded - fan_in
    tail = summed[2 * padded - TAIL :, :]
    loss_sum = jnp.max(tail[0:1, :] + tail[1:2, :])
    count = jnp.max(tail[2:3, :] + tail[3:4, :])
    top = jnp.concatenate(
        [
            summed[fan_in:padded, :],
            summed[padded + fan_in : padded + fan_in + classes - first, :],
            jnp.zeros((LANES - classes, hidden), F32),
        ],
        axis=0,
    )
    g_out[...] = top.T[:, :classes]
    squares = jnp.sum(top * top)
    both = [summed[s * padded : (s + 1) * padded, :].astype(BF16) for s in range(2)]
    grad = mm_nt(both[0], prod[0]) + mm_nt(both[1], prod[1])
    grad = grad[:fan_in, :]
    g_in[...] = grad
    squares += jnp.sum(grad * grad)
    for side in range(2):
        inner = mm(in_t[...], both[side]).astype(BF16)
        grad = mm_nt(inner, cat_b[side * hidden : (side + 1) * hidden, :])
        g_pair[0, side] = grad
        squares += jnp.sum(grad * grad)
        grad = mm(pair_t[side], inner)
        g_cat[0, side * hidden : (side + 1) * hidden, :] = grad
        squares += jnp.sum(grad * grad)
    norm = jnp.sqrt(squares) / count
    factor = (CLIP_AT / jnp.maximum(norm, CLIP_AT)) / count
    loss_out[0] = loss_sum
    count_out[0] = count
    norm_out[0] = norm
    stores = []
    for n, grads in enumerate((g_in, g_pair, g_cat, g_out)):
        w, m, v = bufs[n], bufs[4 + n], bufs[8 + n]
        for k in range(3):
            loads[4 * k + n].wait()
        grad = grads[...] * factor
        first_new = BETA_FIRST * m[...] + (1.0 - BETA_FIRST) * grad
        second_new = BETA_SECOND * v[...] + (1.0 - BETA_SECOND) * grad * grad
        m[...] = first_new
        v[...] = second_new
        first_hat = first_new / (1.0 - BETA_FIRST**ADAM_STEP)
        second_hat = second_new / (1.0 - BETA_SECOND**ADAM_STEP)
        w[...] = w[...] - LEARN_RATE * (
            first_hat / (jnp.sqrt(second_hat) + ADAM_EPS) + WEIGHT_DECAY * w[...]
        )
        for k in range(3):
            store = pltpu.make_async_copy(bufs[4 * k + n], news[4 * k + n], sems_out.at[4 * k + n])
            store.start()
            stores.append(store)
    for store in stores:
        store.wait()


def update(me, got, matrices, states, classes):
    fan_in, hidden = states[0].shape
    padded = matrices[1].shape[1]
    pieces = len(got) // 2
    vmem = pl.BlockSpec(memory_space=pltpu.VMEM)
    smem = pl.BlockSpec(memory_space=pltpu.SMEM)
    hbm = pl.BlockSpec(memory_space=pl.ANY)
    shapes = [jax.ShapeDtypeStruct(s.shape, F32) for s in states]
    return pl.pallas_call(
        functools.partial(update_kernel, (fan_in, classes, pieces)),
        out_shape=shapes + [jax.ShapeDtypeStruct((1,), F32)] * 3,
        in_specs=[smem] + [vmem] * (len(got) + 4) + [hbm] * 12,
        out_specs=[hbm] * 12 + [smem] * 3,
        scratch_shapes=[pltpu.VMEM(s.shape, F32) for s in states]
        + [pltpu.VMEM((2 * padded, hidden), F32)]
        + [pltpu.VMEM(s.shape, F32) for s in states[:4]]
        + [pltpu.SemaphoreType.DMA((12,)), pltpu.SemaphoreType.DMA((12,))],
        compiler_params=pltpu.CompilerParams(vmem_limit_bytes=VMEM_LIMIT),
        name="update",
    )(me, *got, *matrices, *states)


def shards(wide_count, narrow_count, *args):
    features, tile_src, edge_weight, send_lists, labels, train_mask = args[:6]
    states = args[6:18]
    w_in, w_pair, w_cat, w_out = states[:4]
    nodes, fan_in = features.shape
    nb, kt, tile, _ = edge_weight.shape
    classes = w_out.shape[1]
    hidden = w_in.shape[1]
    padded = -(-fan_in // LANES) * LANES
    pieces = wide_count // 2
    piece = padded // pieces
    wide = lax.axis_index("wide")
    me = jnp.stack([wide % 2, wide // 2]).astype(jnp.int32)

    def swap(value, wide_bits, narrow_bits):
        pairs = [
            (w * narrow_count + n, (w ^ wide_bits) * narrow_count + (n ^ narrow_bits))
            for w in range(wide_count)
            for n in range(narrow_count)
        ]
        return lax.ppermute(value, AXES, pairs)

    slots = send_lists.reshape(-1)
    picker = (slots[:, None] == jnp.arange(nodes, dtype=jnp.int32)[None, :]).astype(BF16)
    outgoing = mm(picker, features).astype(BF16)
    outgoing = jnp.pad(outgoing, ((0, 0), (0, padded - fan_in)))
    outgoing = outgoing.reshape(send_lists.shape[1], send_lists.shape[2], padded)
    halo = lax.all_to_all(outgoing, AXES, split_axis=0, concat_axis=0, tiled=True)
    halo = halo.reshape(-1, padded)

    big, prod, in_t, pair_t, cat_b, out_b = weight_products(
        w_in, w_pair[0], w_cat[0], w_out, padded
    )
    keep, send = node_pass(
        tile_src.reshape(-1),
        me,
        features,
        halo,
        edge_weight,
        labels.reshape(nb, tile),
        train_mask.reshape(nb, tile),
        big,
        out_b,
        classes,
        pieces,
    )
    part_b = jax.ShapeDtypeStruct((piece, hidden), BF16)
    part_f = jax.ShapeDtypeStruct((piece, hidden), F32)
    got = swap(send, 1, 0)
    own, *outs = small_call(
        pair_sum_kernel, me, (keep, got), [part_f] + [part_b] * (pieces - 1), "pair_sum"
    )
    got = [swap(outs[d - 1], 2 * d, 0) for d in range(1, pieces)]
    (own,) = small_call(
        functools.partial(plane_sum_kernel, pieces), me, (own, *got), [part_b], "plane_sum"
    )
    got = [swap(own, 0, d) for d in range(1, narrow_count)]
    (own,) = small_call(
        functools.partial(line_sum_kernel, pieces), me, (own, *got), [part_b], "line_sum"
    )
    mine = [own] + [swap(own, 2 * d, 0) for d in range(1, pieces)]
    other = [swap(part, 1, 0) for part in mine]
    results = update(me, mine + other, (prod, in_t, pair_t, cat_b), states, classes)
    return tuple(results[:12]) + tuple(r.reshape(()) for r in results[12:])


def solution(mesh):
    split = P(("wide", "narrow"))
    in_specs = (split,) * 6 + (P(),) * 12
    out_specs = (P(),) * 15
    body = functools.partial(shards, mesh.shape["wide"], mesh.shape["narrow"])
    return jax.shard_map(body, mesh=mesh, in_specs=in_specs, out_specs=out_specs, check_vma=False)
```
